256 devices in a mesh: pb: 16 (over y, z_lo, core), ia: 16 (over z_hi, x).
Axes of the slice: x: 4, y: 4, z: 8 (z_hi: 4, z_lo: 2; z = z_hi * 2 + z_lo), core: 2. Of those that a mesh axis runs over, the one named last changes fastest.
Arguments:
- query_hidden: bfloat16 [32768, 2048], P(('pb', 'ia'))
- item_hidden: bfloat16 [8192, 2048], P(('ia', 'pb'))
- query_weight: bfloat16 [2048, 512], replicated, may hold values from -0.125 to 0.125
- item_weight: bfloat16 [2048, 512], replicated, may hold values from -0.125 to 0.125
- tile_list: int32 [64, 8], P('pb'), may hold values from 0 to 15, all different within a row
- item_counts: int32 [8192], replicated, may hold values from 1 to 4095
- positives: int32 [32768], P('pb'), may hold values from 0 to 8191
Outputs:
- losses: float32 [32768], P(('pb', 'ia'))
- grad_query: float32 [2048, 512], P(('pb', 'ia'))
- grad_item: float32 [2048, 512], P(('pb', 'ia'))
The draws below stay inside these ranges and needn't reach their ends.
Inputs may be any that keep to these rules, and one draw needn't show every extreme that they name: `tile_list`: each row lists 8 different item blocks, and every item block is listed by some row.
All inputs are finite; a program needn't handle non-finite values.
Results may differ from the reference program's by a relative error of at most 0.0044.
Values may be sent and summed in bfloat16 or wider, within the bound.
No kernel may reach another device: no remote copies, remote signals or barrier semaphores. Data moves between devices by JAX's collectives and lax.ppermute only.
A program may use at most 128 MiB of HBM per device.

```python
import math
import jax
import jax.numpy as jnp
from jax import lax

EMBED = 512
TOWER = 2048
BLOCK = 512
IBLK = 1
LISTED = 8
QUERIES = 32768
ITEMS = 8192
N_IA = 16


def tower_draw(key, row_total, salt):
    key = jax.random.fold_in(key, salt)
    base_key, scale_key = jax.random.split(key, 2)
    factor = jnp.exp(jax.random.uniform(scale_key, (row_total, 1), jnp.float32, 0.0, math.log(10.0)))
    base = jax.random.normal(base_key, (row_total, TOWER), jnp.float32)
    return (base * factor).astype(jnp.bfloat16)


def draw_query_hidden(key, part):
    return tower_draw(key, QUERIES, 11)


def draw_item_hidden(key, part):
    return tower_draw(key, ITEMS, 23)


def plant(entries, stream_key, least, top_value):
    place = [jax.random.randint(jax.random.fold_in(stream_key, axis), (), 0, length) for axis, length in enumerate(entries.shape)]
    longest = entries.shape.index(max(entries.shape))
    neighbour = place[:longest] + [(place[longest] + 1) % entries.shape[longest]] + place[longest + 1:]
    return entries.at[tuple(place)].set(least).at[tuple(neighbour)].set(top_value)


def picks_of(rng, rows, count, top, lift):
    order = jax.random.permutation(jax.random.fold_in(rng, 1), count)
    boost = order
    for power in range(3):
        boost = boost * boost // count
    boost = boost * lift // count
    lots = jax.random.randint(jax.random.fold_in(rng, 2), (rows, count), 0, 4096) + boost
    fixed_rows = jax.random.permutation(jax.random.fold_in(rng, 3), rows)[jnp.arange(count) % rows]
    lots = jnp.where(jnp.arange(rows)[:, None] == fixed_rows[None, :], 1 << 14, lots)
    score = lots * count + jnp.arange(count)
    return lax.top_k(score.astype(jnp.int32), top)[1].astype(jnp.int32)


def normal_values(own_key, dims, scale, most, kind=jnp.bfloat16):
    return jnp.clip(scale * jax.random.normal(own_key, dims, jnp.float32), -most, most).astype(kind)


def setup_inputs(seed: int = 0) -> dict:
    key_of = jax.random.split(jax.random.key(seed), 8)
    return {
        "query_hidden": draw_query_hidden(jax.random.fold_in(key_of[7], 71), 0),
        "item_hidden": draw_item_hidden(jax.random.fold_in(key_of[7], 71), 0),
        "query_weight": normal_values(key_of[2], (TOWER, EMBED), TOWER ** -0.5, 0.125),
        "item_weight": normal_values(key_of[3], (TOWER, EMBED), TOWER ** -0.5, 0.125),
        "tile_list": picks_of(key_of[4], (QUERIES // BLOCK), IBLK * N_IA, LISTED, 4096),
        "item_counts": plant(jax.random.randint(key_of[5], (ITEMS,), 1, 4096), jax.random.fold_in(key_of[5], 1), 1, 4095).astype(jnp.int32),
        "positives": plant(jax.random.randint(key_of[6], (QUERIES,), 0, ITEMS), jax.random.fold_in(key_of[6], 1), 0, ITEMS - 1).astype(jnp.int32),
    }


EPS = 1e-06
TEMP = 0.05

def normalize(raw_rows):
    return raw_rows * lax.rsqrt(lax.optimization_barrier(jnp.mean(raw_rows * raw_rows, axis=-1, keepdims=True)) + EPS)

def backnorm(raw_rows, upstream):
    factor = lax.rsqrt(lax.optimization_barrier(jnp.mean(raw_rows * raw_rows, axis=-1, keepdims=True)) + EPS)
    normed = raw_rows * factor
    return factor * (upstream - normed * lax.optimization_barrier(jnp.mean(normed * upstream, axis=-1, keepdims=True)))

def reference(query_hidden, item_hidden, query_weight, item_weight, tile_list, item_counts, positives):
    score_scale = 1.0 / (EMBED * TEMP)
    query_raw = jnp.dot(query_hidden, query_weight, preferred_element_type=jnp.float32)
    item_raw = jnp.dot(item_hidden, item_weight, preferred_element_type=jnp.float32)
    query_unit = normalize(query_raw).astype(jnp.bfloat16)
    item_unit = normalize(item_raw).astype(jnp.bfloat16)
    log_counts = jnp.log(item_counts.astype(jnp.float32))
    query_blocks = QUERIES // BLOCK
    item_tiles = item_unit.reshape(ITEMS // BLOCK, BLOCK, EMBED)
    count_tiles = log_counts.reshape(ITEMS // BLOCK, BLOCK)
    offsets = jnp.arange(BLOCK, dtype=jnp.int32)

    def one_block(item_grad, inputs):
        query_tile, listed, targets = inputs
        gathered = item_tiles[listed].reshape(LISTED * BLOCK, EMBED)
        listed_logs = count_tiles[listed].reshape(LISTED * BLOCK)
        item_ids = (listed[:, None].astype(jnp.int32) * BLOCK + offsets[None, :]).reshape(LISTED * BLOCK).astype(jnp.int32)
        scores = jnp.dot(query_tile, gathered.T, preferred_element_type=jnp.float32) * score_scale - listed_logs[None, :]
        raw_weights = jnp.where(item_ids[None, :] != targets[:, None], jnp.exp(scores), 0.0)
        target_rows = item_unit[targets]
        target_score = lax.optimization_barrier(jnp.sum(query_tile.astype(jnp.float32) * target_rows.astype(jnp.float32), axis=-1)) * score_scale - log_counts[targets]
        target_exp = jnp.exp(target_score)
        totals = lax.optimization_barrier(jnp.sum(raw_weights, axis=1)) + target_exp
        block_losses = jnp.log(totals) - target_score
        weights = (raw_weights / totals[:, None]).astype(jnp.bfloat16)
        coefficient = target_exp / totals - 1.0
        query_grad = (jnp.dot(weights, gathered, preferred_element_type=jnp.float32) + coefficient[:, None] * target_rows.astype(jnp.float32)) * score_scale
        block_grad = jnp.dot(weights.T, query_tile, preferred_element_type=jnp.float32) * score_scale
        item_grad = item_grad.at[item_ids].add(block_grad)
        item_grad = item_grad.at[targets].add(coefficient[:, None] * query_tile.astype(jnp.float32) * score_scale)
        return (item_grad, (block_losses, query_grad))
    item_grad, (losses, query_grad) = lax.scan(one_block, jnp.zeros((ITEMS, EMBED), jnp.float32), (query_unit.reshape(query_blocks, BLOCK, EMBED), tile_list, positives.reshape(query_blocks, BLOCK)))
    query_back = backnorm(query_raw, query_grad.reshape(QUERIES, EMBED)).astype(jnp.bfloat16)
    item_back = backnorm(item_raw, item_grad).astype(jnp.bfloat16)
    grad_query = lax.dot_general(query_hidden, query_back, (((0,), (0,)), ((), ())), preferred_element_type=jnp.float32)
    grad_item = lax.dot_general(item_hidden, item_back, (((0,), (0,)), ((), ())), preferred_element_type=jnp.float32)
    return (losses.reshape(QUERIES), grad_query, grad_item)
```

```python
import functools

import jax
import jax.numpy as jnp
from jax import lax
from jax.experimental import pallas as pl
from jax.experimental.pallas import tpu as pltpu
from jax.sharding import Mesh, PartitionSpec as P

AXES = ("y", "zl", "c", "zh", "x")
EMBED = 512
TOWER = 2048
EPS = 1e-06
TEMP = 0.05
SCALE = 1.0 / (EMBED * TEMP)
BF = jnp.bfloat16
F32 = jnp.float32


def rotation(size, step):
    return [(i, (i + step) % size) for i in range(size)]


def shift(value, step):
    return lax.ppermute(value, "x", rotation(4, step))


def swap(value):
    return lax.ppermute(value, "c", rotation(2, 1))


def spread(value, axes, size):
    return lax.all_to_all(jnp.broadcast_to(value[None], (size,) + value.shape), axes, 0, 0, tiled=True)


VM = functools.partial(pl.BlockSpec, memory_space=pltpu.VMEM)
SM = functools.partial(pl.BlockSpec, memory_space=pltpu.SMEM)


def call(body, outs, ins, scratch=(), flops=0, smem=0):
    return pl.pallas_call(
        body,
        out_shape=tuple(jax.ShapeDtypeStruct(s, d) for s, d in outs),
        in_specs=[SM()] * smem + [VM()] * (len(ins) - smem),
        out_specs=tuple(VM() for _ in outs),
        scratch_shapes=list(scratch),
        compiler_params=pltpu.CompilerParams(vmem_limit_bytes=48 * 1024 * 1024),
        cost_estimate=pl.CostEstimate(flops=flops, bytes_accessed=4 << 20, transcendentals=0),
    )(*ins)


def tower_body(hidden_ref, weight_ref, raw_ref, unit_ref):
    raw = jnp.dot(hidden_ref[...], weight_ref[...], preferred_element_type=F32)
    raw_ref[...] = raw
    unit_ref[...] = (raw * lax.rsqrt(jnp.mean(raw * raw, axis=-1, keepdims=True) + EPS)).astype(BF)


def tower(hidden, weight):
    rows = hidden.shape[0]
    return call(
        tower_body,
        [((rows, EMBED), F32), ((rows, EMBED), BF)],
        [hidden, weight],
        flops=2 * rows * TOWER * EMBED,
    )


def picker(target_x, own_c, relative_c):
    n = lax.broadcasted_iota(jnp.int32, (1, 128), 1)
    k, zh, zl, y_lo = n & 7, (n >> 3) & 3, (n >> 5) & 1, (n >> 6) & 1
    core = own_c if relative_c == 0 else 1 - own_c
    source = ((((y_lo * 2 + zl) * 2 + core) * 4 + zh) * 4 + target_x) * 8 + k
    rows = lax.broadcasted_iota(jnp.int32, (1024, 128), 0)
    return jnp.where(rows == source, 1.0, 0.0).astype(BF)


def pick_columns(hidden_ref, out_ref, target_x, own_c):
    for relative_c in range(2):
        chosen = picker(target_x, own_c, relative_c)
        for y_hi in range(2):
            part = jnp.dot(
                hidden_ref[:, y_hi * 1024 : (y_hi + 1) * 1024], chosen, preferred_element_type=F32
            )
            start = relative_c * 256 + y_hi * 128
            out_ref[:, start : start + 128] = part.astype(BF)


def pick_query_body(place_ref, hidden_ref, *out_refs):
    for step in range(4):
        target_x = lax.rem(place_ref[0] + step, 4)
        pick_columns(hidden_ref, out_refs[step], target_x, place_ref[1])


def pick_item_body(place_ref, h0, h1, h2, h3, out_ref):
    for step, ref in enumerate((h0, h1, h2, h3)):
        pick_columns(ref, out_ref.at[step * 32 : (step + 1) * 32, :], place_ref[0], place_ref[1])


CHUNK = 256


def score_body(place_ref, q0, q1, q2, q3, own_ref, other_ref, logs_ref, listed_ref, hit_ref, exp_ref, sums_ref, query_ref):
    for step, ref in enumerate((q0, q1, q2, q3)):
        at = lax.rem(place_ref[0] + 4 - step, 4) * 128
        query_ref[pl.ds(pl.multiple_of(at, 128), 128), :] = ref[...]
    queries = query_ref[...]
    hit = hit_ref[...]
    total = jnp.zeros((1, 512), F32)
    target = jnp.zeros((1, 512), F32)
    for chunk in range(2048 // CHUNK):
        source, at = (own_ref, chunk * CHUNK) if chunk < 1024 // CHUNK else (other_ref, chunk * CHUNK - 1024)
        items = source[at : at + CHUNK, :]
        rows = slice(chunk * CHUNK, (chunk + 1) * CHUNK)
        dots = lax.dot_general(items, queries, (((1,), (1,)), ((), ())), preferred_element_type=F32)
        scores = dots * SCALE - logs_ref[rows, :]
        ids = lax.broadcasted_iota(jnp.int32, (CHUNK, 512), 0) + chunk * CHUNK
        mine = ids == hit
        live = jnp.where(mine | (listed_ref[rows, :] > 0), jnp.exp(scores), 0.0)
        exp_ref[rows, :] = live.astype(BF)
        total += jnp.sum(live, axis=0, keepdims=True)
        target += jnp.sum(jnp.where(mine, scores, 0.0), axis=0, keepdims=True)
    sums_ref[0:1, :] = total
    sums_ref[1:2, :] = target


def shadow_body(hit_ref, exp_ref, own_ref, other_ref, query_ref, up_ref, hot_ref, pull_ref):
    hit = hit_ref[...]
    queries = query_ref[...]
    for chunk in range(2048 // CHUNK):
        source, at = (own_ref, chunk * CHUNK) if chunk < 1024 // CHUNK else (other_ref, chunk * CHUNK - 1024)
        items = source[at : at + CHUNK, :]
        rows = slice(chunk * CHUNK, (chunk + 1) * CHUNK)
        ids = lax.broadcasted_iota(jnp.int32, (CHUNK, 512), 0) + chunk * CHUNK
        mine = jnp.where(ids == hit, 1.0, 0.0).astype(BF)
        pull_ref[rows, :] = jnp.dot(mine, queries, preferred_element_type=F32)
        up = lax.dot_general(exp_ref[rows, :], items, (((0,), (0,)), ((), ())), preferred_element_type=F32)
        hot = lax.dot_general(mine, items, (((0,), (0,)), ((), ())), preferred_element_type=F32)
        if chunk == 0:
            up_ref[...] = up
            hot_ref[...] = hot
        else:
            up_ref[...] += up
            hot_ref[...] += hot


def inverse_column(s0, s1, s2, s3):
    total = s0[0:1, :] + s1[0:1, :] + s2[0:1, :] + s3[0:1, :]
    inverse = jnp.broadcast_to(1.0 / total, (128, 512))
    return jnp.transpose(inverse)[:, 0:1]


def item_grad_body(s0, s1, s2, s3, exp_ref, query_ref, pull_ref, keep_ref, send_ref):
    scaled = (query_ref[...].astype(F32) * inverse_column(s0, s1, s2, s3)).astype(BF)
    for chunk in range(2048 // CHUNK):
        rows = slice(chunk * CHUNK, (chunk + 1) * CHUNK)
        part = jnp.dot(exp_ref[rows, :], scaled, preferred_element_type=F32) - pull_ref[rows, :]
        if chunk < 1024 // CHUNK:
            keep_ref[rows, :] = part
        else:
            send_ref[rows.start - 1024 : rows.stop - 1024, :] = part.astype(BF)


def query_grad_body(place_ref, s0, s1, s2, s3, up_ref, hot_ref, loss_ref, own_ref, v1, v2, v3):
    inverse = inverse_column(s0, s1, s2, s3)
    total = s0[0:1, :] + s1[0:1, :] + s2[0:1, :] + s3[0:1, :]
    target = s0[1:2, :] + s1[1:2, :] + s2[1:2, :] + s3[1:2, :]
    loss_ref[...] = jnp.log(total) - target
    up_ref_value = up_ref[...] * inverse - hot_ref[...]
    hot_ref[...] = up_ref_value
    for step, ref in enumerate((own_ref, v1, v2, v3)):
        at = pl.multiple_of(lax.rem(place_ref[0] + step, 4) * 128, 128)
        ref[...] = hot_ref[pl.ds(at, 128), :].astype(ref.dtype)


def back_body(raw_ref, *refs):
    out_ref = refs[-1]
    grad = refs[0][...].astype(F32)
    for ref in refs[1:-1]:
        grad = grad + ref[...].astype(F32)
    grad = grad * SCALE
    raw = raw_ref[...]
    factor = lax.rsqrt(jnp.mean(raw * raw, axis=-1, keepdims=True) + EPS)
    unit = raw * factor
    out_ref[...] = (factor * (grad - unit * jnp.mean(unit * grad, axis=-1, keepdims=True))).astype(BF)


def back_stack_body(raw_ref, grads_ref, out_ref):
    grad = grads_ref[0].astype(F32)
    for part in range(1, grads_ref.shape[0]):
        grad = grad + grads_ref[part].astype(F32)
    grad = grad * SCALE
    raw = raw_ref[...]
    factor = lax.rsqrt(jnp.mean(raw * raw, axis=-1, keepdims=True) + EPS)
    unit = raw * factor
    out_ref[...] = (factor * (grad - unit * jnp.mean(unit * grad, axis=-1, keepdims=True))).astype(BF)


def last_body(*refs):
    hq, bq, hi, bi, (keep_ref, send_ref) = refs[0:4], refs[4:8], refs[8], refs[9:13], refs[13:15]
    query = item = None
    for step in range(4):
        part = lax.dot_general(hq[step][...], bq[step][...], (((0,), (0,)), ((), ())), preferred_element_type=F32)
        query = part if query is None else query + part
        part = lax.dot_general(
            hi[step * 32 : (step + 1) * 32, :], bi[step][...], (((0,), (0,)), ((), ())), preferred_element_type=F32
        )
        item = part if item is None else item + part
    keep_ref[:, 0:EMBED] = query[0:256]
    keep_ref[:, EMBED:] = item[0:256]
    send_ref[:, 0:EMBED] = query[256:512].astype(BF)
    send_ref[:, EMBED:] = item[256:512].astype(BF)


def add_body(a_ref, b_ref, out_ref):
    out_ref[...] = (a_ref[...].astype(F32) + b_ref[...].astype(F32)).astype(out_ref.dtype)


def add(a, b, dtype):
    return call(add_body, [(a.shape, dtype)], [a, b])[0]


def add_stack_body(parts_ref, out_ref):
    total = parts_ref[0].astype(F32)
    for part in range(1, parts_ref.shape[0]):
        total = total + parts_ref[part].astype(F32)
    out_ref[...] = total.astype(out_ref.dtype)


def add_stack(parts, dtype):
    return call(add_stack_body, [(parts.shape[1:], dtype)], [parts])[0]


def local(query_hidden, item_hidden, query_weight, item_weight, tile_list, item_counts, positives):
    my_x, my_c, my_zh = lax.axis_index("x"), lax.axis_index("c"), lax.axis_index("zh")
    place = jnp.stack([my_x, my_c]).astype(jnp.int32)

    item_raw, item_unit = tower(item_hidden, item_weight)
    query_raw, query_unit = tower(query_hidden, query_weight)
    queries = [query_unit] + [shift(query_unit, k) for k in (1, 2, 3)]

    z_items = spread(item_unit, ("zl", "zh"), 8)
    own_items = spread(z_items.reshape(256, EMBED), "y", 4).reshape(1024, EMBED)
    other_items = swap(own_items)

    hidden_items = [item_hidden] + [shift(item_hidden, k) for k in (1, 2, 3)]
    picked = call(
        pick_query_body, [((128, EMBED), BF)] * 4, [place, query_hidden], smem=1, flops=2 * 128 * 2048 * 512
    )
    hidden_queries = [picked[0]] + [shift(picked[k], k) for k in (1, 2, 3)]
    hidden_items = call(
        pick_item_body, [((128, EMBED), BF)], [place] + hidden_items, smem=1, flops=2 * 128 * 1024 * 512
    )[0]

    counts = item_counts.reshape(4, 4, 4, 2, 2, 32)
    counts = lax.dynamic_index_in_dim(counts, my_x, 1, keepdims=False)
    counts = counts.transpose(3, 1, 2, 0, 4)
    counts = jnp.where(my_c == 0, counts, counts[::-1])
    logs = jnp.log(counts.astype(F32)).reshape(2048, 1)
    row_list = lax.dynamic_index_in_dim(tile_list, my_zh, 0, keepdims=False)
    blocks = jnp.arange(4, dtype=jnp.int32) * 4 + my_x
    listed = jnp.any(row_list[None, :] == blocks[:, None], axis=1)
    listed = jnp.broadcast_to(listed.astype(F32)[None, :, None], (16, 4, 32)).reshape(2048, 1)
    wanted = lax.dynamic_slice_in_dim(positives, my_zh * 512, 512, 0).reshape(1, 512)
    block, within = wanted >> 9, wanted & 511
    order = ((((within >> 5) & 1) ^ my_c) << 10) | ((within >> 6) << 7) | ((block >> 2) << 5) | (within & 31)
    hit = jnp.where((block & 3) == my_x, order, -1)

    exps, sums, query_rows = call(
        score_body,
        [((2048, 512), BF), ((2, 512), F32), ((512, EMBED), BF)],
        [place, *queries, own_items, other_items, logs, listed, hit],
        smem=1,
        flops=2 * 2048 * 512 * 512,
    )
    all_sums = [sums] + [shift(sums, k) for k in (1, 2, 3)]
    up, hot, pull = call(
        shadow_body,
        [((512, EMBED), F32), ((512, EMBED), F32), ((2048, EMBED), F32)],
        [hit, exps, own_items, other_items, query_rows],
        flops=6 * 2048 * 512 * 512,
    )
    keep, send = call(
        item_grad_body,
        [((1024, EMBED), F32), ((1024, EMBED), BF)],
        [*all_sums, exps, query_rows, pull],
        flops=2 * 2048 * 512 * 512,
    )
    came = swap(send)
    losses, v0, v1, v2, v3 = call(
        query_grad_body,
        [((1, 512), F32), ((128, EMBED), F32)] + [((128, EMBED), BF)] * 3,
        [place, *all_sums, up, hot],
        smem=1,
        flops=1 << 20,
    )
    losses = lax.dynamic_slice_in_dim(losses.reshape(512), my_x * 128, 128, 0)
    query_parts = [v0, shift(v1, 1), shift(v2, 2), shift(v3, 3)]
    query_back = call(back_body, [((128, EMBED), BF)], [query_raw, *query_parts])[0]
    query_backs = [query_back] + [shift(query_back, k) for k in (1, 2, 3)]

    item_part = add(keep, came, BF)
    item_part = lax.all_to_all(item_part.reshape(4, 256, EMBED), "y", 0, 0, tiled=True)
    item_part = add_stack(item_part, BF)
    item_part = lax.all_to_all(item_part.reshape(8, 32, EMBED), ("zl", "zh"), 0, 0, tiled=True)
    item_back = call(back_stack_body, [((32, EMBED), BF)], [item_raw, item_part])[0]
    item_backs = [item_back] + [shift(item_back, k) for k in (1, 2, 3)]

    keep, send = call(
        last_body,
        [((256, 2 * EMBED), F32), ((256, 2 * EMBED), BF)],
        [*hidden_queries, *query_backs, hidden_items, *item_backs],
        flops=2 * 640 * 512 * 512,
    )
    part = add(keep, swap(send), BF)
    part = lax.all_to_all(part.reshape(4, 64, 2 * EMBED), "y", 0, 0, tiled=True)
    part = add_stack(part, BF)
    part = lax.all_to_all(part.reshape(8, 8, 2 * EMBED), ("zl", "zh"), 0, 0, tiled=True)
    grads = add_stack(part, F32)
    return (losses, grads[:, :EMBED], grads[:, EMBED:])


def solution(mesh):
    inner = Mesh(mesh.devices.reshape(4, 2, 2, 4, 4), AXES)
    pb, ia = ("y", "zl", "c"), ("zh", "x")
    placed = (P(pb + ia, None), P(ia + pb, None), P(), P(), P(pb, None), P(), P(pb))
    return jax.shard_map(
        local,
        mesh=inner,
        in_specs=placed,
        out_specs=(P(pb + ia), P(pb + ia, None), P(pb + ia, None)),
        check_vma=False,
    )
```

```python
import functools

import jax
import jax.numpy as jnp
from jax import lax
from jax.experimental import pallas as pl
from jax.experimental.pallas import tpu as pltpu
from jax.sharding import Mesh, PartitionSpec as P

AXES = ("y", "zl", "c", "zh", "x")
EMBED = 512
TOWER = 2048
EPS = 1e-06
TEMP = 0.05
SCALE = 1.0 / (EMBED * TEMP)
BF = jnp.bfloat16
F32 = jnp.float32
I32 = jnp.int32
SLOTS = [(d, k) for d in range(2) for k in range(4)]


def shift(value, step, axis="x"):
    return lax.ppermute(value, axis, [(i, (i + step) % 4) for i in range(4)])


def around(value, axis="x"):
    return [value] + [shift(value, k, axis) for k in (1, 2, 3)]


def both_cores(value):
    return jnp.concatenate([value, swap(value)], axis=0)


def slots(value):
    return around(both_cores(value))


def after(value, *others):
    return lax.optimization_barrier((value, *others))[0]


def swap(value):
    return lax.ppermute(value, "c", [(0, 1), (1, 0)])


VM = functools.partial(pl.BlockSpec, memory_space=pltpu.VMEM)
SM = functools.partial(pl.BlockSpec, memory_space=pltpu.SMEM)


def call(body, outs, ins, scratch=(), flops=1 << 20, smem=0, moved=1 << 20):
    return pl.pallas_call(
        body,
        out_shape=tuple(jax.ShapeDtypeStruct(s, d) for s, d in outs),
        in_specs=[SM()] * smem + [VM()] * (len(ins) - smem),
        out_specs=tuple(VM() for _ in outs),
        scratch_shapes=list(scratch),
        compiler_params=pltpu.CompilerParams(vmem_limit_bytes=16 * 1024 * 1024),
        cost_estimate=pl.CostEstimate(flops=flops, bytes_accessed=moved, transcendentals=0),
    )(*ins)


def to_unit(raw):
    return (raw * lax.rsqrt(jnp.mean(raw * raw, axis=-1, keepdims=True) + EPS)).astype(BF)


def item_tower_body(hidden_hbm, weight_hbm, unit_ref, hidden, weight, sems):
    part = TOWER // 4
    copies = [pltpu.make_async_copy(hidden_hbm, hidden, sems.at[4])]
    for i in range(4):
        rows = pl.ds(i * part, part)
        copies.append(pltpu.make_async_copy(weight_hbm.at[rows], weight.at[rows], sems.at[i]))
    for copy in copies:
        copy.start()
    copies[0].wait()
    raw = None
    for i in range(4):
        copies[i + 1].wait()
        rows = slice(i * part, (i + 1) * part)
        term = jnp.dot(hidden[:, rows], weight[rows, :], preferred_element_type=F32)
        raw = term if raw is None else raw + term
    unit_ref[...] = jnp.broadcast_to(to_unit(raw)[None], unit_ref.shape)


def item_tower(hidden, weight):
    hbm = pl.BlockSpec(memory_space=pltpu.HBM)
    return pl.pallas_call(
        item_tower_body,
        out_shape=jax.ShapeDtypeStruct((8, 32, EMBED), BF),
        in_specs=[hbm, hbm],
        out_specs=VM(),
        scratch_shapes=[
            pltpu.VMEM((32, TOWER), BF),
            pltpu.VMEM((TOWER, EMBED), BF),
            pltpu.SemaphoreType.DMA((5,)),
        ],
        compiler_params=pltpu.CompilerParams(vmem_limit_bytes=60 * 1024 * 1024),
        cost_estimate=pl.CostEstimate(flops=2 * 32 * TOWER * EMBED, bytes_accessed=2 << 20, transcendentals=0),
    )(hidden, weight)


def item_raw_body(hidden_ref, weight_ref, raw_ref):
    raw_ref[...] = jnp.dot(hidden_ref[...], weight_ref[...], preferred_element_type=F32)


def query_tower_body(place_ref, hidden_ref, weight_ref, counts_ref, raw_ref, unit_ref, logs_ref, rows):
    raw = jnp.dot(hidden_ref[...], weight_ref[...], preferred_element_type=F32)
    raw_ref[...] = raw
    unit_ref[...] = to_unit(raw)
    rows[...] = jnp.ones_like(rows)
    for back in range(4):
        for zh in range(4):
            at = zh * 16 + place_ref[0] * 4 + lax.rem(place_ref[3] + 4 - back, 4)
            rows[back * 4 + zh : back * 4 + zh + 1, :] = counts_ref[pl.ds(at, 1), :].astype(F32)
    logs_ref[...] = jnp.transpose(jnp.log(rows[...]))


def pick_body(place_ref, query_ref, item_ref, *refs):
    own_refs, other_ref, both = refs[0:4], refs[4], refs[5]
    both[0:128, :] = query_ref[...]
    both[128:160, :] = item_ref[...]
    lane = lax.broadcasted_iota(I32, (1, 256), 1)
    n = lane & 127
    k, zh, zl, y_lo = n & 7, (n >> 3) & 3, (n >> 5) & 1, (n >> 6) & 1
    rows = lax.broadcasted_iota(I32, (1024, 256), 0)
    c = place_ref[1] ^ (lane >> 7)
    for forward in range(4):
        x = lax.rem(place_ref[0] + forward, 4)
        source = ((((y_lo * 2 + zl) * 2 + c) * 4 + zh) * 4 + x) * 8 + k
        chosen = jnp.where(rows == source, 1.0, 0.0).astype(BF)
        for y_hi in range(2):
            lanes = slice(y_hi * 128, (y_hi + 1) * 128)
            part = jnp.dot(
                both[:, y_hi * 1024 : (y_hi + 1) * 1024], chosen, preferred_element_type=F32
            ).astype(BF)
            own_refs[forward][:, lanes] = part[:, 0:128]
            other_ref[forward, :, lanes] = part[:, 128:256]


def hits_of(place_ref, own_positives, other_positives):
    x, c, zh, y = place_ref[0], place_ref[1], place_ref[2], place_ref[3]
    hits = []
    for d, k in SLOTS:
        ref = own_positives if d == 0 else other_positives
        wanted = ref[pl.ds(zh * 4 + lax.rem(x + 4 - k, 4), 1), :]
        block, within = wanted >> 9, wanted & 511
        back = (y + 4 - (within >> 7)) & 3
        row = (back << 8) | (((within >> 6) & 1) << 7) | ((block >> 2) << 5) | (within & 31)
        hits.append(jnp.where(((block & 3) == x) & (((within >> 5) & 1) == c), row, -1))
    return jnp.concatenate(hits, axis=1)


def score_body(place_ref, own_tiles, other_tiles, *refs):
    q_refs, i_refs, (logs_ref, own_positives, other_positives) = refs[0:4], refs[4:8], refs[8:11]
    exp_ref, sums_ref, query_ref, hit_ref = refs[11:15]
    for s, (d, k) in enumerate(SLOTS):
        query_ref[s * 128 : (s + 1) * 128, :] = q_refs[k][d * 128 : (d + 1) * 128, :]
    queries = query_ref[...]
    hit = hits_of(place_ref, own_positives, other_positives)
    hit_ref[...] = hit
    x, c, zh = place_ref[0], place_ref[1], place_ref[2]
    block_of_row = lax.broadcasted_iota(I32, (128, 1), 0) >> 5
    listed = []
    for tiles in (own_tiles, other_tiles):
        flags = jnp.zeros((128, 1), I32)
        for z in range(4):
            flag = jnp.int32(0)
            for entry in range(8):
                flag = flag | (tiles[zh, entry] == z * 4 + x).astype(I32)
            flags = jnp.where(block_of_row == z, flag, flags)
        listed.append(jnp.broadcast_to(flags, (128, 512)))
    listed = jnp.concatenate(listed, axis=1) > 0
    total = jnp.zeros((1, 1024), F32)
    target = jnp.zeros((1, 1024), F32)
    ids = lax.broadcasted_iota(I32, (128, 1024), 0)
    for y, items_ref in enumerate(i_refs):
        for zl in range(2):
            first = (y * 2 + zl) * 128
            items = items_ref[zl * 128 : (zl + 1) * 128, :]
            dots = lax.dot_general(items, queries, (((1,), (1,)), ((), ())), preferred_element_type=F32)
            at = pl.multiple_of(zl * 64 + c * 32, 32)
            logs = jnp.concatenate([logs_ref[pl.ds(at, 32), y * 4 + z : y * 4 + z + 1] for z in range(4)], axis=0)
            scores = dots * SCALE - logs
            mine = ids == hit - first
            live = jnp.where(mine | listed, jnp.exp(scores), 0.0)
            exp_ref[first : first + 128, :] = live.astype(BF)
            total += jnp.sum(live, axis=0, keepdims=True)
            target += jnp.sum(jnp.where(mine, scores, 0.0), axis=0, keepdims=True)
    for s in range(8):
        sums_ref[s : s + 1, :] = total[:, s * 128 : (s + 1) * 128]
        sums_ref[8 + s : 9 + s, :] = target[:, s * 128 : (s + 1) * 128]


CHUNK = 256


def shadow_body(hit_ref, exp_ref, i0, i1, i2, i3, query_ref, up_ref, hot_ref, pull_ref):
    hit = hit_ref[...]
    for chunk, items_ref in enumerate((i0, i1, i2, i3)):
        rows = slice(chunk * CHUNK, (chunk + 1) * CHUNK)
        ids = lax.broadcasted_iota(I32, (CHUNK, 1024), 0) + chunk * CHUNK
        mine = jnp.where(ids == hit, 1.0, 0.0).astype(BF)
        pull_ref[rows, :] = jnp.dot(mine, query_ref[...], preferred_element_type=F32)
        items = items_ref[...]
        up = lax.dot_general(exp_ref[rows, :], items, (((0,), (0,)), ((), ())), preferred_element_type=F32)
        hot = lax.dot_general(mine, items, (((0,), (0,)), ((), ())), preferred_element_type=F32)
        if chunk == 0:
            up_ref[...] = up
            hot_ref[...] = hot
        else:
            up_ref[...] += up
            hot_ref[...] += hot


def full_sums(refs, start):
    out = []
    for d, k in SLOTS:
        total = None
        for step in range(4):
            for flip in range(2):
                s = start + (d ^ flip) * 4 + (k - step) % 4
                part = refs[step][flip * 16 + s : flip * 16 + s + 1, :]
                total = part if total is None else total + part
        out.append(total)
    return jnp.concatenate(out, axis=1)


def inverse_column(total):
    return jnp.transpose(jnp.broadcast_to(1.0 / total, (128, 1024)))[:, 0:1]


def item_grad_body(s0, s1, s2, s3, exp_ref, query_ref, pull_ref, g0, g1, g2, g3):
    inverse = inverse_column(full_sums((s0, s1, s2, s3), 0))
    scaled = (query_ref[...].astype(F32) * inverse).astype(BF)
    for chunk, out_ref in enumerate((g0, g1, g2, g3)):
        rows = slice(chunk * CHUNK, (chunk + 1) * CHUNK)
        part = jnp.dot(exp_ref[rows, :], scaled, preferred_element_type=F32) - pull_ref[rows, :]
        out_ref[...] = part.astype(out_ref.dtype)


def query_grad_body(s0, s1, s2, s3, up_ref, hot_ref, loss_ref, keep_ref, send_ref):
    sums = (s0, s1, s2, s3)
    total = full_sums(sums, 0)
    inverse = inverse_column(total)
    loss_ref[...] = jnp.log(total[:, 0:128]) - full_sums(sums, 8)[:, 0:128]
    keep_ref[...] = up_ref[0:512, :] * inverse[0:512] - hot_ref[0:512, :]
    send_ref[...] = (up_ref[512:1024, :] * inverse[512:1024] - hot_ref[512:1024, :]).astype(BF)


def query_fold_body(keep_ref, came_ref, p0, p1, p2, p3, other_ref, grad_ref, o0, o1, o2, o3):
    for s, (picked_ref, ref) in enumerate(((p0, o0), (p1, o1), (p2, o2), (p3, o3))):
        rows = slice((4 - s) % 4 * 128, (4 - s) % 4 * 128 + 128)
        grad = keep_ref[rows, :] + came_ref[rows, :].astype(F32)
        if s == 0:
            grad_ref[...] = grad
        else:
            ref[0:128, :] = grad.astype(BF)
        ref[128:288, 0:256] = picked_ref[...]
        ref[128:288, 256:512] = other_ref[s]


def to_back(raw, grad):
    grad = grad * SCALE
    factor = lax.rsqrt(jnp.mean(raw * raw, axis=-1, keepdims=True) + EPS)
    unit = raw * factor
    return (factor * (grad - unit * jnp.mean(unit * grad, axis=-1, keepdims=True))).astype(BF)


def query_back_body(raw_ref, own_ref, v1, v2, v3, out_ref):
    grad = own_ref[...]
    for ref in (v1, v2, v3):
        grad = grad + ref[0:128, :].astype(F32)
    out_ref[...] = to_back(raw_ref[...], grad)


def item_back_body(raw_ref, grads_ref, out_ref):
    grad = grads_ref[0].astype(F32)
    for part in range(1, grads_ref.shape[0]):
        grad = grad + grads_ref[part].astype(F32)
    out_ref[...] = to_back(raw_ref[...], grad)


def last_query_body(h0, h1, h2, h3, *refs):
    hidden_refs, total = (h0, h1, h2, h3), None
    for s, (d, k) in enumerate(SLOTS):
        part = lax.dot_general(
            hidden_refs[k][128:256, d * 256 : (d + 1) * 256], refs[s][...], (((0,), (0,)), ((), ())), preferred_element_type=F32
        )
        total = part if total is None else total + part
    refs[8][...] = total


def last_item_body(place_ref, h0, h1, h2, h3, b0, b1, b2, b3, query_ref, o0, o1, o2, o3, item):
    hidden_refs, back_refs, total = (h0, h1, h2, h3), (b0, b1, b2, b3), None
    for d, k in SLOTS:
        part = lax.dot_general(
            hidden_refs[k][256:288, d * 256 : (d + 1) * 256],
            back_refs[k][d * 32 : (d + 1) * 32, :],
            (((0,), (0,)), ((), ())),
            preferred_element_type=F32,
        )
        total = part if total is None else total + part
    item[...] = total
    for back, out_ref in enumerate((o0, o1, o2, o3)):
        at = pl.multiple_of(lax.rem(place_ref[3] + 4 - back, 4) * 64, 64)
        out_ref[:, 0:EMBED] = query_ref[pl.ds(at, 64), :].astype(out_ref.dtype)
        out_ref[:, EMBED:] = item[pl.ds(at, 64), :].astype(out_ref.dtype)


def add_body(own_ref, p1, p2, p3, out_ref):
    total = own_ref[...] + p1[...].astype(F32) + p2[...].astype(F32) + p3[...].astype(F32)
    out_ref[...] = total.astype(BF).reshape(out_ref.shape)


def scatter_y(parts, shape):
    came = [shift(parts[k], 4 - k, "y") for k in (1, 2, 3)]
    return call(add_body, [(shape, BF)], [parts[0], *came])[0]


def split_body(parts_ref, query_ref, item_ref):
    total = parts_ref[0].astype(F32)
    for part in range(1, parts_ref.shape[0]):
        total = total + parts_ref[part].astype(F32)
    query_ref[...] = total[:, 0:EMBED]
    item_ref[...] = total[:, EMBED:]


def local(query_hidden, item_hidden, query_weight, item_weight, tile_list, item_counts, positives):
    place = jnp.stack([lax.axis_index(axis) for axis in ("x", "c", "zh", "y")]).astype(I32)
    counts = item_counts.reshape(64, 128)
    own_positives = positives.reshape(16, 128)

    item_units = item_tower(item_hidden, item_weight)
    z_items = lax.all_to_all(item_units, ("zl", "zh"), 0, 0, tiled=True).reshape(256, EMBED)

    query_raw, query_unit, logs = call(
        query_tower_body,
        [((128, EMBED), F32), ((128, EMBED), BF), ((128, 128), F32)],
        [place, after(query_hidden, item_units), query_weight, counts],
        scratch=[pltpu.VMEM((128, 128), F32)],
        smem=1,
        flops=1,
        moved=1,
    )
    queries = slots(query_unit)
    picked = call(
        pick_body,
        [((160, 256), BF)] * 4 + [((4, 160, 256), BF)],
        [place, query_hidden, after(item_hidden, query_unit)],
        scratch=[pltpu.VMEM((160, TOWER), BF)],
        smem=1,
        flops=1,
        moved=1,
    )
    z_items = after(z_items, query_unit, picked[4])
    other_picked = swap(after(picked[4], z_items))
    items = around(z_items, "y")

    own_positives, tile_list = after((own_positives, tile_list), z_items)
    other_positives = swap(own_positives)
    other_tiles = swap(tile_list)
    exps, sums, query_rows, hit = call(
        score_body,
        [((1024, 1024), BF), ((16, 128), F32), ((1024, EMBED), BF), ((1, 1024), I32)],
        [place, tile_list, other_tiles, *queries, *items, logs, own_positives, other_positives],
        smem=3,
        flops=2 * 1024 * 1024 * 512,
    )
    all_sums = around(both_cores(sums))
    up, hot, pull = call(
        shadow_body,
        [((1024, EMBED), F32), ((1024, EMBED), F32), ((1024, EMBED), F32)],
        [hit, exps, *items, query_rows],
        flops=6 * 1024 * 1024 * 512,
    )
    item_parts = call(
        item_grad_body,
        [((256, EMBED), F32)] + [((256, EMBED), BF)] * 3,
        [*all_sums, exps, query_rows, pull],
        flops=2 * 1024 * 1024 * 512,
    )
    item_part = scatter_y(item_parts, (8, 32, EMBED))

    losses, keep, send = call(
        query_grad_body,
        [((1, 128), F32), ((512, EMBED), F32), ((512, EMBED), BF)],
        [*all_sums, up, after(hot, item_parts[3])],
        moved=16 << 20,
    )
    own_grad, *hidden = call(
        query_fold_body,
        [((128, EMBED), F32)] + [((288, EMBED), BF)] * 4,
        [keep, swap(send), *picked[0:4], other_picked],
    )
    hidden = [hidden[0]] + [shift(hidden[k], k) for k in (1, 2, 3)]
    query_back = call(query_back_body, [((128, EMBED), BF)], [query_raw, own_grad, *hidden[1:]])[0]
    query_backs = around(query_back)
    query_backs = query_backs + [swap(part) for part in query_backs]
    query_last = call(
        last_query_body,
        [((256, EMBED), F32)],
        [*hidden, *query_backs],
        flops=2 * 1024 * 256 * 512,
        moved=4 << 20,
    )[0]

    item_part = after(item_part, query_back)
    item_raw = call(
        item_raw_body,
        [((32, EMBED), F32)],
        [after(item_hidden, item_part), item_weight],
        flops=2 * 32 * TOWER * EMBED,
    )[0]
    item_part = lax.all_to_all(item_part, ("zl", "zh"), 0, 0, tiled=True)
    item_back = call(item_back_body, [((32, EMBED), BF)], [item_raw, item_part])[0]
    item_backs = slots(item_back)

    parts = call(
        last_item_body,
        [((64, 2 * EMBED), F32)] + [((64, 2 * EMBED), BF)] * 3,
        [place, *hidden, *item_backs, query_last],
        scratch=[pltpu.VMEM((256, EMBED), F32)],
        smem=1,
        flops=2 * 256 * 256 * 512,
    )
    part = scatter_y(parts, (8, 8, 2 * EMBED))
    part = lax.all_to_all(part, ("zl", "zh"), 0, 0, tiled=True)
    grad_query, grad_item = call(split_body, [((8, EMBED), F32)] * 2, [part])
    return (losses.reshape(128), grad_query, grad_item)


def solution(mesh):
    inner = Mesh(mesh.devices.reshape(4, 2, 2, 4, 4), AXES)
    pb, ia = ("y", "zl", "c"), ("zh", "x")
    placed = (P(pb + ia, None), P(ia + pb, None), P(), P(), P(pb, None), P(), P(pb))
    return jax.shard_map(
        local,
        mesh=inner,
        in_specs=placed,
        out_specs=(P(pb + ia), P(pb + ia, None), P(pb + ia, None)),
        check_vma=False,
    )
```

```python
import functools

import jax
import jax.numpy as jnp
from jax import lax
from jax.experimental import pallas as pl
from jax.experimental.pallas import tpu as pltpu
from jax.sharding import Mesh, PartitionSpec as P

AXES = ("y", "zl", "c", "zh", "x")
EMBED = 512
TOWER = 2048
EPS = 1e-06
TEMP = 0.05
SCALE = 1.0 / (EMBED * TEMP)
BF = jnp.bfloat16
F32 = jnp.float32
I32 = jnp.int32
SLOTS = [(d, k) for d in range(2) for k in range(4)]


def shift(value, step, axis="x"):
    return lax.ppermute(value, axis, [(i, (i + step) % 4) for i in range(4)])


def around(value, axis="x"):
    return [value] + [shift(value, k, axis) for k in (1, 2, 3)]


def both_cores(value):
    return jnp.concatenate([value, swap(value)], axis=0)


def slots(value):
    return around(both_cores(value))


def after(value, *others):
    return lax.optimization_barrier((value, *others))[0]


def swap(value):
    return lax.ppermute(value, "c", [(0, 1), (1, 0)])


VM = functools.partial(pl.BlockSpec, memory_space=pltpu.VMEM)
SM = functools.partial(pl.BlockSpec, memory_space=pltpu.SMEM)


def call(body, outs, ins, scratch=(), flops=1 << 20, smem=0, moved=1 << 20):
    return pl.pallas_call(
        body,
        out_shape=tuple(jax.ShapeDtypeStruct(s, d) for s, d in outs),
        in_specs=[SM()] * smem + [VM()] * (len(ins) - smem),
        out_specs=tuple(VM() for _ in outs),
        scratch_shapes=list(scratch),
        compiler_params=pltpu.CompilerParams(vmem_limit_bytes=16 * 1024 * 1024),
        cost_estimate=pl.CostEstimate(flops=flops, bytes_accessed=moved, transcendentals=0),
    )(*ins)


def to_unit(raw):
    return (raw * lax.rsqrt(jnp.mean(raw * raw, axis=-1, keepdims=True) + EPS)).astype(BF)


def item_tower_body(hidden_hbm, weight_hbm, unit_ref, hidden, weight, sems):
    part = TOWER // 4
    copies = [pltpu.make_async_copy(hidden_hbm, hidden, sems.at[4])]
    for i in range(4):
        rows = pl.ds(i * part, part)
        copies.append(pltpu.make_async_copy(weight_hbm.at[rows], weight.at[rows], sems.at[i]))
    for copy in copies:
        copy.start()
    copies[0].wait()
    raw = None
    for i in range(4):
        copies[i + 1].wait()
        rows = slice(i * part, (i + 1) * part)
        term = jnp.dot(hidden[:, rows], weight[rows, :], preferred_element_type=F32)
        raw = term if raw is None else raw + term
    unit_ref[...] = jnp.broadcast_to(to_unit(raw)[None], unit_ref.shape)


def item_tower(hidden, weight):
    hbm = pl.BlockSpec(memory_space=pltpu.HBM)
    return pl.pallas_call(
        item_tower_body,
        out_shape=jax.ShapeDtypeStruct((8, 32, EMBED), BF),
        in_specs=[hbm, hbm],
        out_specs=VM(),
        scratch_shapes=[
            pltpu.VMEM((32, TOWER), BF),
            pltpu.VMEM((TOWER, EMBED), BF),
            pltpu.SemaphoreType.DMA((5,)),
        ],
        compiler_params=pltpu.CompilerParams(vmem_limit_bytes=60 * 1024 * 1024),
        cost_estimate=pl.CostEstimate(flops=2 * 32 * TOWER * EMBED, bytes_accessed=2 << 20, transcendentals=0),
    )(hidden, weight)


def item_raw_body(hidden_ref, weight_ref, raw_ref):
    raw_ref[...] = jnp.dot(hidden_ref[...], weight_ref[...], preferred_element_type=F32)


def query_tower_body(place_ref, hidden_ref, weight_ref, counts_ref, raw_ref, unit_ref, logs_ref, rows):
    raw = jnp.dot(hidden_ref[...], weight_ref[...], preferred_element_type=F32)
    raw_ref[...] = raw
    unit_ref[...] = to_unit(raw)
    rows[...] = jnp.ones_like(rows)
    for back in range(4):
        for zh in range(4):
            at = zh * 16 + place_ref[0] * 4 + lax.rem(place_ref[3] + 4 - back, 4)
            rows[back * 4 + zh : back * 4 + zh + 1, :] = counts_ref[pl.ds(at, 1), :].astype(F32)
    logs_ref[...] = jnp.transpose(jnp.log(rows[...]))


def pick_body(place_ref, query_ref, item_ref, *refs):
    own_refs, other_ref, both = refs[0:4], refs[4], refs[5]
    both[0:128, :] = query_ref[...]
    both[128:160, :] = item_ref[...]
    lane = lax.broadcasted_iota(I32, (1, 256), 1)
    n = lane & 127
    k, zh, zl, y_lo = n & 7, (n >> 3) & 3, (n >> 5) & 1, (n >> 6) & 1
    rows = lax.broadcasted_iota(I32, (1024, 256), 0)
    c = place_ref[1] ^ (lane >> 7)
    for forward in range(4):
        x = lax.rem(place_ref[0] + forward, 4)
        source = ((((y_lo * 2 + zl) * 2 + c) * 4 + zh) * 4 + x) * 8 + k
        chosen = jnp.where(rows == source, 1.0, 0.0).astype(BF)
        for y_hi in range(2):
            lanes = slice(y_hi * 128, (y_hi + 1) * 128)
            part = jnp.dot(
                both[:, y_hi * 1024 : (y_hi + 1) * 1024], chosen, preferred_element_type=F32
            ).astype(BF)
            own_refs[forward][:, lanes] = part[:, 0:128]
            other_ref[forward, :, lanes] = part[:, 128:256]


def hits_of(place_ref, own_positives, other_positives):
    x, c, zh, y = place_ref[0], place_ref[1], place_ref[2], place_ref[3]
    hits = []
    for d, k in SLOTS:
        ref = own_positives if d == 0 else other_positives
        wanted = ref[pl.ds(zh * 4 + lax.rem(x + 4 - k, 4), 1), :]
        block, within = wanted >> 9, wanted & 511
        back = (y + 4 - (within >> 7)) & 3
        row = (back << 8) | (((within >> 6) & 1) << 7) | ((block >> 2) << 5) | (within & 31)
        hits.append(jnp.where(((block & 3) == x) & (((within >> 5) & 1) == c), row, -1))
    return jnp.concatenate(hits, axis=1)


def score_body(place_ref, own_tiles, other_tiles, *refs):
    q_refs, i_refs, (logs_ref, own_positives, other_positives) = refs[0:8], refs[8:12], refs[12:15]
    exp_ref, sums_ref, query_ref, hit_ref = refs[15:19]
    for s, ref in enumerate(q_refs):
        query_ref[s * 128 : (s + 1) * 128, :] = ref[...]
    queries = query_ref[...]
    hit = hits_of(place_ref, own_positives, other_positives)
    hit_ref[...] = hit
    x, c, zh = place_ref[0], place_ref[1], place_ref[2]
    block_of_row = lax.broadcasted_iota(I32, (128, 1), 0) >> 5
    listed = []
    for tiles in (own_tiles, other_tiles):
        flags = jnp.zeros((128, 1), I32)
        for z in range(4):
            flag = jnp.int32(0)
            for entry in range(8):
                flag = flag | (tiles[zh, entry] == z * 4 + x).astype(I32)
            flags = jnp.where(block_of_row == z, flag, flags)
        listed.append(jnp.broadcast_to(flags, (128, 512)))
    listed = jnp.concatenate(listed, axis=1) > 0
    total = jnp.zeros((1, 1024), F32)
    target = jnp.zeros((1, 1024), F32)
    ids = lax.broadcasted_iota(I32, (128, 1024), 0)
    for y, items_ref in enumerate(i_refs):
        for zl in range(2):
            first = (y * 2 + zl) * 128
            items = items_ref[zl * 128 : (zl + 1) * 128, :]
            dots = lax.dot_general(items, queries, (((1,), (1,)), ((), ())), preferred_element_type=F32)
            at = pl.multiple_of(zl * 64 + c * 32, 32)
            logs = jnp.concatenate([logs_ref[pl.ds(at, 32), y * 4 + z : y * 4 + z + 1] for z in range(4)], axis=0)
            scores = dots * SCALE - logs
            mine = ids == hit - first
            live = jnp.where(mine | listed, jnp.exp(scores), 0.0)
            exp_ref[first : first + 128, :] = live.astype(BF)
            total += jnp.sum(live, axis=0, keepdims=True)
            target += jnp.sum(jnp.where(mine, scores, 0.0), axis=0, keepdims=True)
    for s in range(8):
        sums_ref[s : s + 1, :] = total[:, s * 128 : (s + 1) * 128]
        sums_ref[8 + s : 9 + s, :] = target[:, s * 128 : (s + 1) * 128]


CHUNK = 256


def shadow_body(hit_ref, exp_ref, i0, i1, i2, i3, query_ref, up_ref, hot_ref, pull_ref):
    hit = hit_ref[...]
    for chunk, items_ref in enumerate((i0, i1, i2, i3)):
        rows = slice(chunk * CHUNK, (chunk + 1) * CHUNK)
        ids = lax.broadcasted_iota(I32, (CHUNK, 1024), 0) + chunk * CHUNK
        mine = jnp.where(ids == hit, 1.0, 0.0).astype(BF)
        pull_ref[rows, :] = jnp.dot(mine, query_ref[...], preferred_element_type=F32)
        items = items_ref[...]
        up = lax.dot_general(exp_ref[rows, :], items, (((0,), (0,)), ((), ())), preferred_element_type=F32)
        hot = lax.dot_general(mine, items, (((0,), (0,)), ((), ())), preferred_element_type=F32)
        if chunk == 0:
            up_ref[...] = up
            hot_ref[...] = hot
        else:
            up_ref[...] += up
            hot_ref[...] += hot


def full_sums(refs, start):
    out = []
    for d, k in SLOTS:
        total = None
        for step in range(4):
            for flip in range(2):
                s = start + (d ^ flip) * 4 + (k - step) % 4
                part = refs[step][flip * 16 + s : flip * 16 + s + 1, :]
                total = part if total is None else total + part
        out.append(total)
    return jnp.concatenate(out, axis=1)


def inverse_column(total):
    return jnp.transpose(jnp.broadcast_to(1.0 / total, (128, 1024)))[:, 0:1]


def item_grad_body(s0, s1, s2, s3, exp_ref, query_ref, pull_ref, g0, g1, g2, g3):
    inverse = inverse_column(full_sums((s0, s1, s2, s3), 0))
    scaled = (query_ref[...].astype(F32) * inverse).astype(BF)
    for chunk, out_ref in enumerate((g0, g1, g2, g3)):
        rows = slice(chunk * CHUNK, (chunk + 1) * CHUNK)
        part = jnp.dot(exp_ref[rows, :], scaled, preferred_element_type=F32) - pull_ref[rows, :]
        out_ref[...] = part.astype(out_ref.dtype)


def query_grad_body(s0, s1, s2, s3, up_ref, hot_ref, loss_ref, keep_ref, send_ref):
    sums = (s0, s1, s2, s3)
    total = full_sums(sums, 0)
    inverse = inverse_column(total)
    loss_ref[...] = jnp.log(total[:, 0:128]) - full_sums(sums, 8)[:, 0:128]
    keep_ref[...] = up_ref[0:512, :] * inverse[0:512] - hot_ref[0:512, :]
    send_ref[...] = (up_ref[512:1024, :] * inverse[512:1024] - hot_ref[512:1024, :]).astype(BF)


def query_fold_body(keep_ref, came_ref, p0, p1, p2, p3, other_ref, grad_ref, o0, o1, o2, o3):
    for s, (picked_ref, ref) in enumerate(((p0, o0), (p1, o1), (p2, o2), (p3, o3))):
        rows = slice((4 - s) % 4 * 128, (4 - s) % 4 * 128 + 128)
        grad = keep_ref[rows, :] + came_ref[rows, :].astype(F32)
        if s == 0:
            grad_ref[...] = grad
        else:
            ref[0:128, :] = grad.astype(BF)
        ref[128:288, 0:256] = picked_ref[...]
        ref[128:288, 256:512] = other_ref[s]


def to_back(raw, grad):
    grad = grad * SCALE
    factor = lax.rsqrt(jnp.mean(raw * raw, axis=-1, keepdims=True) + EPS)
    unit = raw * factor
    return (factor * (grad - unit * jnp.mean(unit * grad, axis=-1, keepdims=True))).astype(BF)


def query_back_body(raw_ref, own_ref, v1, v2, v3, out_ref):
    grad = own_ref[...]
    for ref in (v1, v2, v3):
        grad = grad + ref[0:128, :].astype(F32)
    out_ref[...] = to_back(raw_ref[...], grad)


def item_back_body(raw_ref, grads_ref, out_ref):
    grad = grads_ref[0].astype(F32)
    for part in range(1, grads_ref.shape[0]):
        grad = grad + grads_ref[part].astype(F32)
    out_ref[...] = to_back(raw_ref[...], grad)


def last_query_body(h0, h1, h2, h3, *refs):
    hidden_refs, total = (h0, h1, h2, h3), None
    for s, (d, k) in enumerate(SLOTS):
        part = lax.dot_general(
            hidden_refs[k][128:256, d * 256 : (d + 1) * 256], refs[s][...], (((0,), (0,)), ((), ())), preferred_element_type=F32
        )
        total = part if total is None else total + part
    refs[8][...] = total


def last_item_body(place_ref, h0, h1, h2, h3, b0, b1, b2, b3, query_ref, o0, o1, o2, o3, item):
    hidden_refs, back_refs, total = (h0, h1, h2, h3), (b0, b1, b2, b3), None
    for d, k in SLOTS:
        part = lax.dot_general(
            hidden_refs[k][256:288, d * 256 : (d + 1) * 256],
            back_refs[k][d * 32 : (d + 1) * 32, :],
            (((0,), (0,)), ((), ())),
            preferred_element_type=F32,
        )
        total = part if total is None else total + part
    item[...] = total
    for back, out_ref in enumerate((o0, o1, o2, o3)):
        at = pl.multiple_of(lax.rem(place_ref[3] + 4 - back, 4) * 64, 64)
        out_ref[:, 0:EMBED] = query_ref[pl.ds(at, 64), :].astype(out_ref.dtype)
        out_ref[:, EMBED:] = item[pl.ds(at, 64), :].astype(out_ref.dtype)


def add_body(own_ref, p1, p2, p3, out_ref):
    total = own_ref[...] + p1[...].astype(F32) + p2[...].astype(F32) + p3[...].astype(F32)
    out_ref[...] = total.astype(BF).reshape(out_ref.shape)


def scatter_y(parts, shape):
    came = [shift(parts[k], 4 - k, "y") for k in (1, 2, 3)]
    return call(add_body, [(shape, BF)], [parts[0], *came])[0]


def split_body(parts_ref, query_ref, item_ref):
    total = parts_ref[0].astype(F32)
    for part in range(1, parts_ref.shape[0]):
        total = total + parts_ref[part].astype(F32)
    query_ref[...] = total[:, 0:EMBED]
    item_ref[...] = total[:, EMBED:]


def local(query_hidden, item_hidden, query_weight, item_weight, tile_list, item_counts, positives):
    place = jnp.stack([lax.axis_index(axis) for axis in ("x", "c", "zh", "y")]).astype(I32)
    counts = item_counts.reshape(64, 128)
    own_positives = positives.reshape(16, 128)

    item_units = item_tower(item_hidden, item_weight)
    z_items = lax.all_to_all(item_units, ("zl", "zh"), 0, 0, tiled=True).reshape(256, EMBED)

    query_raw, query_unit, logs = call(
        query_tower_body,
        [((128, EMBED), F32), ((128, EMBED), BF), ((128, 128), F32)],
        [place, after(query_hidden, item_units), query_weight, counts],
        scratch=[pltpu.VMEM((128, 128), F32)],
        smem=1,
        flops=1,
        moved=1,
    )
    queries = around(query_unit)
    picked = call(
        pick_body,
        [((160, 256), BF)] * 4 + [((4, 160, 256), BF)],
        [place, query_hidden, after(item_hidden, query_unit)],
        scratch=[pltpu.VMEM((160, TOWER), BF)],
        smem=1,
        flops=1,
        moved=1,
    )
    z_items = after(z_items, query_unit, picked[4])
    other_picked = swap(after(picked[4], z_items))
    items = around(z_items, "y")
    queries = queries + [swap(after(part, z_items)) for part in queries]

    own_positives, tile_list = after((own_positives, tile_list), z_items)
    other_positives = swap(own_positives)
    other_tiles = swap(tile_list)
    exps, sums, query_rows, hit = call(
        score_body,
        [((1024, 1024), BF), ((16, 128), F32), ((1024, EMBED), BF), ((1, 1024), I32)],
        [place, tile_list, other_tiles, *queries, *items, logs, own_positives, other_positives],
        smem=3,
        flops=2 * 1024 * 1024 * 512,
    )
    all_sums = around(both_cores(sums))
    up, hot, pull = call(
        shadow_body,
        [((1024, EMBED), F32), ((1024, EMBED), F32), ((1024, EMBED), F32)],
        [hit, exps, *items, query_rows],
        flops=6 * 1024 * 1024 * 512,
    )
    item_parts = call(
        item_grad_body,
        [((256, EMBED), F32)] + [((256, EMBED), BF)] * 3,
        [*all_sums, exps, query_rows, after(pull, other_picked)],
        flops=2 * 1024 * 1024 * 512,
    )
    item_part = scatter_y(item_parts, (8, 32, EMBED))

    losses, keep, send = call(
        query_grad_body,
        [((1, 128), F32), ((512, EMBED), F32), ((512, EMBED), BF)],
        [*all_sums, up, after(hot, item_parts[3])],
        moved=16 << 20,
    )
    own_grad, *hidden = call(
        query_fold_body,
        [((128, EMBED), F32)] + [((288, EMBED), BF)] * 4,
        [keep, swap(send), *picked[0:4], other_picked],
    )
    hidden = [hidden[0]] + [shift(hidden[k], k) for k in (1, 2, 3)]
    query_back = call(query_back_body, [((128, EMBED), BF)], [query_raw, own_grad, *hidden[1:]])[0]
    query_backs = around(query_back)
    query_backs = query_backs + [swap(part) for part in query_backs]
    query_last = call(
        last_query_body,
        [((256, EMBED), F32)],
        [*hidden, *query_backs],
        flops=2 * 1024 * 256 * 512,
        moved=4 << 20,
    )[0]

    item_part = after(item_part, query_back)
    item_raw = call(
        item_raw_body,
        [((32, EMBED), F32)],
        [after(item_hidden, item_part), item_weight],
        flops=2 * 32 * TOWER * EMBED,
    )[0]
    item_part = lax.all_to_all(item_part, ("zl", "zh"), 0, 0, tiled=True)
    item_back = call(item_back_body, [((32, EMBED), BF)], [item_raw, item_part])[0]
    item_backs = slots(item_back)

    parts = call(
        last_item_body,
        [((64, 2 * EMBED), F32)] + [((64, 2 * EMBED), BF)] * 3,
        [place, *hidden, *item_backs, query_last],
        scratch=[pltpu.VMEM((256, EMBED), F32)],
        smem=1,
        flops=2 * 256 * 256 * 512,
    )
    part = scatter_y(parts, (8, 8, 2 * EMBED))
    part = lax.all_to_all(part, ("zl", "zh"), 0, 0, tiled=True)
    grad_query, grad_item = call(split_body, [((8, EMBED), F32)] * 2, [part])
    return (losses.reshape(128), grad_query, grad_item)


def solution(mesh):
    inner = Mesh(mesh.devices.reshape(4, 2, 2, 4, 4), AXES)
    pb, ia = ("y", "zl", "c"), ("zh", "x")
    placed = (P(pb + ia, None), P(ia + pb, None), P(), P(), P(pb, None), P(), P(pb))
    return jax.shard_map(
        local,
        mesh=inner,
        in_specs=placed,
        out_specs=(P(pb + ia), P(pb + ia, None), P(pb + ia, None)),
        check_vma=False,
    )
```

```python
import functools

import jax
import jax.numpy as jnp
from jax import lax
from jax.experimental import pallas as pl
from jax.experimental.pallas import tpu as pltpu
from jax.sharding import Mesh, PartitionSpec as P

AXES = ("y", "zl", "c", "zh", "x")
EMBED = 512
TOWER = 2048
EPS = 1e-06
TEMP = 0.05
SCALE = 1.0 / (EMBED * TEMP)
BF = jnp.bfloat16
F32 = jnp.float32
I32 = jnp.int32
SLOTS = [(d, k) for d in range(2) for k in range(4)]


def shift(value, step, axis="x"):
    return lax.ppermute(value, axis, [(i, (i + step) % 4) for i in range(4)])


def around(value, axis="x"):
    return [value] + [shift(value, k, axis) for k in (1, 2, 3)]


def both_cores(value):
    return jnp.concatenate([value, swap(value)], axis=0)


def slots(value):
    return around(both_cores(value))


def after(value, *others):
    return lax.optimization_barrier((value, *others))[0]


def swap(value):
    return lax.ppermute(value, "c", [(0, 1), (1, 0)])


VM = functools.partial(pl.BlockSpec, memory_space=pltpu.VMEM)
SM = functools.partial(pl.BlockSpec, memory_space=pltpu.SMEM)


def call(body, outs, ins, scratch=(), flops=1 << 20, smem=0, moved=1 << 20, limit=16):
    return pl.pallas_call(
        body,
        out_shape=tuple(jax.ShapeDtypeStruct(s, d) for s, d in outs),
        in_specs=[SM()] * smem + [VM()] * (len(ins) - smem),
        out_specs=tuple(VM() for _ in outs),
        scratch_shapes=list(scratch),
        compiler_params=pltpu.CompilerParams(vmem_limit_bytes=limit * 1024 * 1024),
        cost_estimate=pl.CostEstimate(flops=flops, bytes_accessed=moved, transcendentals=0),
    )(*ins)


def to_unit(raw):
    return (raw * lax.rsqrt(jnp.mean(raw * raw, axis=-1, keepdims=True) + EPS)).astype(BF)


def item_tower_body(hidden_hbm, weight_hbm, unit_ref, hidden, weight, sems):
    part = TOWER // 4
    copies = [pltpu.make_async_copy(hidden_hbm, hidden, sems.at[4])]
    for i in range(4):
        rows = pl.ds(i * part, part)
        copies.append(pltpu.make_async_copy(weight_hbm.at[rows], weight.at[rows], sems.at[i]))
    for copy in copies:
        copy.start()
    copies[0].wait()
    raw = None
    for i in range(4):
        copies[i + 1].wait()
        rows = slice(i * part, (i + 1) * part)
        term = jnp.dot(hidden[:, rows], weight[rows, :], preferred_element_type=F32)
        raw = term if raw is None else raw + term
    unit_ref[...] = jnp.broadcast_to(to_unit(raw)[None], unit_ref.shape)


def item_tower(hidden, weight):
    hbm = pl.BlockSpec(memory_space=pltpu.HBM)
    return pl.pallas_call(
        item_tower_body,
        out_shape=jax.ShapeDtypeStruct((8, 32, EMBED), BF),
        in_specs=[hbm, hbm],
        out_specs=VM(),
        scratch_shapes=[
            pltpu.VMEM((32, TOWER), BF),
            pltpu.VMEM((TOWER, EMBED), BF),
            pltpu.SemaphoreType.DMA((5,)),
        ],
        compiler_params=pltpu.CompilerParams(vmem_limit_bytes=60 * 1024 * 1024),
        cost_estimate=pl.CostEstimate(flops=2 * 32 * TOWER * EMBED, bytes_accessed=2 << 20, transcendentals=0),
    )(hidden, weight)


def item_raw_body(hidden_ref, weight_ref, raw_ref):
    raw_ref[...] = jnp.dot(hidden_ref[...], weight_ref[...], preferred_element_type=F32)


def query_tower_body(place_ref, hidden_ref, weight_ref, counts_ref, raw_ref, unit_ref, logs_ref, rows):
    raw = jnp.dot(hidden_ref[...], weight_ref[...], preferred_element_type=F32)
    raw_ref[...] = raw
    unit_ref[...] = to_unit(raw)
    rows[...] = jnp.ones_like(rows)
    for back in range(4):
        for zh in range(4):
            at = zh * 16 + place_ref[0] * 4 + lax.rem(place_ref[3] + 4 - back, 4)
            rows[back * 4 + zh : back * 4 + zh + 1, :] = counts_ref[pl.ds(at, 1), :].astype(F32)
    logs_ref[...] = jnp.transpose(jnp.log(rows[...]))


def pick_body(place_ref, query_ref, item_ref, *refs):
    own_refs, other_ref, both = refs[0:4], refs[4], refs[5]
    both[0:128, :] = query_ref[...]
    both[128:160, :] = item_ref[...]
    lane = lax.broadcasted_iota(I32, (1, 256), 1)
    n = lane & 127
    k, zh, zl, y_lo = n & 7, (n >> 3) & 3, (n >> 5) & 1, (n >> 6) & 1
    rows = lax.broadcasted_iota(I32, (1024, 256), 0)
    c = place_ref[1] ^ (lane >> 7)
    for forward in range(4):
        x = lax.rem(place_ref[0] + forward, 4)
        source = ((((y_lo * 2 + zl) * 2 + c) * 4 + zh) * 4 + x) * 8 + k
        chosen = jnp.where(rows == source, 1.0, 0.0).astype(BF)
        for y_hi in range(2):
            lanes = slice(y_hi * 128, (y_hi + 1) * 128)
            part = jnp.dot(
                both[:, y_hi * 1024 : (y_hi + 1) * 1024], chosen, preferred_element_type=F32
            ).astype(BF)
            own_refs[forward][:, lanes] = part[:, 0:128]
            other_ref[forward, :, lanes] = part[:, 128:256]


def hits_of(place_ref, own_positives, other_positives):
    x, c, zh, y = place_ref[0], place_ref[1], place_ref[2], place_ref[3]
    hits = []
    for d, k in SLOTS:
        ref = own_positives if d == 0 else other_positives
        wanted = ref[pl.ds(zh * 4 + lax.rem(x + 4 - k, 4), 1), :]
        block, within = wanted >> 9, wanted & 511
        back = (y + 4 - (within >> 7)) & 3
        row = (back << 8) | (((within >> 6) & 1) << 7) | ((block >> 2) << 5) | (within & 31)
        hits.append(jnp.where(((block & 3) == x) & (((within >> 5) & 1) == c), row, -1))
    return jnp.concatenate(hits, axis=1)


def score_body(place_ref, own_tiles, other_tiles, *refs):
    q_refs, i_refs, (logs_ref, own_positives, other_positives) = refs[0:4], refs[4:8], refs[8:11]
    exp_ref, sums_ref, query_ref, hit_ref = refs[11:15]
    for s, (d, k) in enumerate(SLOTS):
        query_ref[s * 128 : (s + 1) * 128, :] = q_refs[k][d * 128 : (d + 1) * 128, :]
    queries = query_ref[...]
    hit = hits_of(place_ref, own_positives, other_positives)
    hit_ref[...] = hit
    x, c, zh = place_ref[0], place_ref[1], place_ref[2]
    block_of_row = lax.broadcasted_iota(I32, (128, 1), 0) >> 5
    listed = []
    for tiles in (own_tiles, other_tiles):
        flags = jnp.zeros((128, 1), I32)
        for z in range(4):
            flag = jnp.int32(0)
            for entry in range(8):
                flag = flag | (tiles[zh, entry] == z * 4 + x).astype(I32)
            flags = jnp.where(block_of_row == z, flag, flags)
        listed.append(jnp.broadcast_to(flags, (128, 512)))
    listed = jnp.concatenate(listed, axis=1) > 0
    total = jnp.zeros((1, 1024), F32)
    target = jnp.zeros((1, 1024), F32)
    ids = lax.broadcasted_iota(I32, (128, 1024), 0)
    for y, items_ref in enumerate(i_refs):
        for zl in range(2):
            first = (y * 2 + zl) * 128
            items = items_ref[zl * 128 : (zl + 1) * 128, :]
            dots = lax.dot_general(items, queries, (((1,), (1,)), ((), ())), preferred_element_type=F32)
            at = pl.multiple_of(zl * 64 + c * 32, 32)
            logs = jnp.concatenate([logs_ref[pl.ds(at, 32), y * 4 + z : y * 4 + z + 1] for z in range(4)], axis=0)
            scores = dots * SCALE - logs
            mine = ids == hit - first
            live = jnp.where(mine | listed, jnp.exp(scores), 0.0)
            exp_ref[first : first + 128, :] = live.astype(BF)
            total += jnp.sum(live, axis=0, keepdims=True)
            target += jnp.sum(jnp.where(mine, scores, 0.0), axis=0, keepdims=True)
    for s in range(8):
        sums_ref[s : s + 1, :] = total[:, s * 128 : (s + 1) * 128]
        sums_ref[8 + s : 9 + s, :] = target[:, s * 128 : (s + 1) * 128]


CHUNK = 256


def shadow_body(hit_ref, exp_ref, i0, i1, i2, i3, query_ref, up_ref, hot_ref, pull_ref):
    hit = hit_ref[...]
    for chunk, items_ref in enumerate((i0, i1, i2, i3)):
        rows = slice(chunk * CHUNK, (chunk + 1) * CHUNK)
        ids = lax.broadcasted_iota(I32, (CHUNK, 1024), 0) + chunk * CHUNK
        mine = jnp.where(ids == hit, 1.0, 0.0).astype(BF)
        pull_ref[rows, :] = jnp.dot(mine, query_ref[...], preferred_element_type=F32)
        items = items_ref[...]
        up = lax.dot_general(exp_ref[rows, :], items, (((0,), (0,)), ((), ())), preferred_element_type=F32)
        hot = lax.dot_general(mine, items, (((0,), (0,)), ((), ())), preferred_element_type=F32)
        if chunk == 0:
            up_ref[...] = up
            hot_ref[...] = hot
        else:
            up_ref[...] += up
            hot_ref[...] += hot


def full_sums(refs, start):
    out = []
    for d, k in SLOTS:
        total = None
        for step in range(4):
            for flip in range(2):
                s = start + (d ^ flip) * 4 + (k - step) % 4
                part = refs[step][flip * 16 + s : flip * 16 + s + 1, :]
                total = part if total is None else total + part
        out.append(total)
    return jnp.concatenate(out, axis=1)


def inverse_column(total):
    return jnp.transpose(jnp.broadcast_to(1.0 / total, (128, 1024)))[:, 0:1]


def item_grad_body(s0, s1, s2, s3, exp_ref, query_ref, pull_ref, g0, g1, g2, g3):
    inverse = inverse_column(full_sums((s0, s1, s2, s3), 0))
    scaled = (query_ref[...].astype(F32) * inverse).astype(BF)
    for chunk, out_ref in enumerate((g0, g1, g2, g3)):
        rows = slice(chunk * CHUNK, (chunk + 1) * CHUNK)
        part = jnp.dot(exp_ref[rows, :], scaled, preferred_element_type=F32) - pull_ref[rows, :]
        out_ref[...] = part.astype(out_ref.dtype)


def query_grad_body(s0, s1, s2, s3, up_ref, hot_ref, loss_ref, keep_ref, send_ref):
    sums = (s0, s1, s2, s3)
    total = full_sums(sums, 0)
    inverse = inverse_column(total)
    loss_ref[...] = jnp.log(total[:, 0:128]) - full_sums(sums, 8)[:, 0:128]
    keep_ref[...] = up_ref[0:512, :] * inverse[0:512] - hot_ref[0:512, :]
    send_ref[...] = (up_ref[512:1024, :] * inverse[512:1024] - hot_ref[512:1024, :]).astype(BF)


def query_fold_body(keep_ref, came_ref, p0, p1, p2, p3, other_ref, grad_ref, o0, o1, o2, o3):
    for s, (picked_ref, ref) in enumerate(((p0, o0), (p1, o1), (p2, o2), (p3, o3))):
        rows = slice((4 - s) % 4 * 128, (4 - s) % 4 * 128 + 128)
        grad = keep_ref[rows, :] + came_ref[rows, :].astype(F32)
        if s == 0:
            grad_ref[...] = grad
        else:
            ref[0:128, :] = grad.astype(BF)
        ref[128:288, 0:256] = picked_ref[...]
        ref[128:288, 256:512] = other_ref[s]


def to_back(raw, grad):
    grad = grad * SCALE
    factor = lax.rsqrt(jnp.mean(raw * raw, axis=-1, keepdims=True) + EPS)
    unit = raw * factor
    return (factor * (grad - unit * jnp.mean(unit * grad, axis=-1, keepdims=True))).astype(BF)


def query_back_body(raw_ref, own_ref, v1, v2, v3, out_ref):
    grad = own_ref[...]
    for ref in (v1, v2, v3):
        grad = grad + ref[0:128, :].astype(F32)
    out_ref[...] = to_back(raw_ref[...], grad)


def item_back_body(raw_ref, grads_ref, out_ref):
    grad = grads_ref[0].astype(F32)
    for part in range(1, grads_ref.shape[0]):
        grad = grad + grads_ref[part].astype(F32)
    out_ref[...] = to_back(raw_ref[...], grad)


def last_query_body(h0, h1, h2, h3, *refs):
    hidden_refs, total = (h0, h1, h2, h3), None
    for s, (d, k) in enumerate(SLOTS):
        part = lax.dot_general(
            hidden_refs[k][128:256, d * 256 : (d + 1) * 256], refs[s][...], (((0,), (0,)), ((), ())), preferred_element_type=F32
        )
        total = part if total is None else total + part
    refs[8][...] = total


def last_item_body(place_ref, h0, h1, h2, h3, b0, b1, b2, b3, query_ref, o0, o1, o2, o3, item):
    hidden_refs, back_refs, total = (h0, h1, h2, h3), (b0, b1, b2, b3), None
    for d, k in SLOTS:
        part = lax.dot_general(
            hidden_refs[k][256:288, d * 256 : (d + 1) * 256],
            back_refs[k][d * 32 : (d + 1) * 32, :],
            (((0,), (0,)), ((), ())),
            preferred_element_type=F32,
        )
        total = part if total is None else total + part
    item[...] = total
    for back, out_ref in enumerate((o0, o1, o2, o3)):
        at = pl.multiple_of(lax.rem(place_ref[3] + 4 - back, 4) * 64, 64)
        out_ref[:, 0:EMBED] = query_ref[pl.ds(at, 64), :].astype(out_ref.dtype)
        out_ref[:, EMBED:] = item[pl.ds(at, 64), :].astype(out_ref.dtype)


def add_body(own_ref, p1, p2, p3, out_ref):
    total = own_ref[...] + p1[...].astype(F32) + p2[...].astype(F32) + p3[...].astype(F32)
    out_ref[...] = total.astype(BF).reshape(out_ref.shape)


def scatter_y(parts, shape, limit=16):
    came = [shift(parts[k], 4 - k, "y") for k in (1, 2, 3)]
    return call(add_body, [(shape, BF)], [parts[0], *came], limit=limit)[0]


def split_body(parts_ref, query_ref, item_ref):
    total = parts_ref[0].astype(F32)
    for part in range(1, parts_ref.shape[0]):
        total = total + parts_ref[part].astype(F32)
    query_ref[...] = total[:, 0:EMBED]
    item_ref[...] = total[:, EMBED:]


def local(query_hidden, item_hidden, query_weight, item_weight, tile_list, item_counts, positives):
    place = jnp.stack([lax.axis_index(axis) for axis in ("x", "c", "zh", "y")]).astype(I32)
    counts = item_counts.reshape(64, 128)
    own_positives = positives.reshape(16, 128)

    item_units = item_tower(item_hidden, item_weight)
    z_items = lax.all_to_all(item_units, ("zl", "zh"), 0, 0, tiled=True).reshape(256, EMBED)

    query_raw, query_unit, logs = call(
        query_tower_body,
        [((128, EMBED), F32), ((128, EMBED), BF), ((128, 128), F32)],
        [place, after(query_hidden, item_units), query_weight, counts],
        scratch=[pltpu.VMEM((128, 128), F32)],
        smem=1,
        flops=1,
        moved=1,
    )
    queries = slots(query_unit)
    picked = call(
        pick_body,
        [((160, 256), BF)] * 4 + [((4, 160, 256), BF)],
        [place, query_hidden, after(item_hidden, query_unit)],
        scratch=[pltpu.VMEM((160, TOWER), BF)],
        smem=1,
        flops=1,
        moved=1,
    )
    z_items = after(z_items, query_unit, picked[4])
    other_picked = swap(after(picked[4], z_items))
    items = around(z_items, "y")

    own_positives, tile_list = after((own_positives, tile_list), z_items)
    other_positives = swap(own_positives)
    other_tiles = swap(tile_list)
    exps, sums, query_rows, hit = call(
        score_body,
        [((1024, 1024), BF), ((16, 128), F32), ((1024, EMBED), BF), ((1, 1024), I32)],
        [place, tile_list, other_tiles, *queries, *items, logs, own_positives, other_positives],
        smem=3,
        flops=2 * 1024 * 1024 * 512,
    )
    all_sums = around(both_cores(sums))
    up, hot, pull = call(
        shadow_body,
        [((1024, EMBED), F32), ((1024, EMBED), F32), ((1024, EMBED), F32)],
        [hit, exps, *items, query_rows],
        flops=6 * 1024 * 1024 * 512,
    )
    item_parts = call(
        item_grad_body,
        [((256, EMBED), F32)] + [((256, EMBED), BF)] * 3,
        [*all_sums, exps, query_rows, pull],
        flops=2 * 1024 * 1024 * 512,
    )
    item_part = scatter_y(item_parts, (8, 32, EMBED))

    losses, keep, send = call(
        query_grad_body,
        [((1, 128), F32), ((512, EMBED), F32), ((512, EMBED), BF)],
        [*all_sums, up, after(hot, item_parts[3])],
        moved=16 << 20,
    )
    own_grad, *hidden = call(
        query_fold_body,
        [((128, EMBED), F32)] + [((288, EMBED), BF)] * 4,
        [keep, swap(send), *picked[0:4], other_picked],
    )
    hidden = [hidden[0]] + [shift(hidden[k], k) for k in (1, 2, 3)]
    query_back = call(query_back_body, [((128, EMBED), BF)], [query_raw, own_grad, *hidden[1:]])[0]
    query_backs = around(query_back)
    query_backs = query_backs + [swap(part) for part in query_backs]
    query_last = call(
        last_query_body,
        [((256, EMBED), F32)],
        [*hidden, *query_backs],
        flops=2 * 1024 * 256 * 512,
        moved=4 << 20,
    )[0]

    item_part = after(item_part, query_back)
    item_raw = call(
        item_raw_body,
        [((32, EMBED), F32)],
        [after(item_hidden, item_part), item_weight],
        flops=2 * 32 * TOWER * EMBED,
    )[0]
    item_part = lax.all_to_all(item_part, ("zl", "zh"), 0, 0, tiled=True)
    item_back = call(item_back_body, [((32, EMBED), BF)], [item_raw, item_part], limit=60)[0]
    item_backs = slots(item_back)

    parts = call(
        last_item_body,
        [((64, 2 * EMBED), F32)] + [((64, 2 * EMBED), BF)] * 3,
        [place, *hidden, *item_backs, query_last],
        scratch=[pltpu.VMEM((256, EMBED), F32)],
        smem=1,
        flops=2 * 256 * 256 * 512,
    )
    part = scatter_y(parts, (8, 8, 2 * EMBED))
    part = lax.all_to_all(part, ("zl", "zh"), 0, 0, tiled=True)
    grad_query, grad_item = call(split_body, [((8, EMBED), F32)] * 2, [part])
    return (losses.reshape(128), grad_query, grad_item)


def solution(mesh):
    inner = Mesh(mesh.devices.reshape(4, 2, 2, 4, 4), AXES)
    pb, ia = ("y", "zl", "c"), ("zh", "x")
    placed = (P(pb + ia, None), P(ia + pb, None), P(), P(), P(pb, None), P(), P(pb))
    return jax.shard_map(
        local,
        mesh=inner,
        in_specs=placed,
        out_specs=(P(pb + ia), P(pb + ia, None), P(pb + ia, None)),
        check_vma=False,
    )
```
